32 devices in a mesh: groups: 2 (over y), wide: 8 (over z, x), narrow: 2 (over core).
Axes of the slice: x: 2, y: 2, z: 4, core: 2. Of those that a mesh axis runs over, the one named last changes fastest.
Arguments:
- new_tokens: bfloat16 [4096, 8192], P(('groups', 'wide')), parts along dimension 0, may hold values from -6 to 6
- kv_weight: bfloat16 [8192, 1024], P('wide', 'narrow'), may hold values from -0.0625 to 0.0625
- prefix_cache: bfloat16 [2, 2048, 1024], P(None, ('groups', 'wide'), 'narrow'), parts along dimension 1, may hold values from -6 to 6
- queries: bfloat16 [16, 4096], P(('groups', 'wide'), 'narrow'), parts along dimension 0, may hold values from -64 to 64
- doc_of_question: int32 [16], P('groups'), parts along dimension 0, may hold values from 0 to 1
- span_lists: int32 [16, 8], P('groups'), parts along dimension 0, may hold values from 0 to 3
- span_slot: int32 [8], P('groups'), parts along dimension 0, may hold values from 0 to 3, each once
Outputs:
- new_cache: bfloat16 [4096, 1024], P(('groups', 'wide'), 'narrow'), parts along dimension 0
- attended: bfloat16 [16, 4096], P(('groups', 'wide'), 'narrow'), parts along dimension 0
The draws below stay inside these ranges and needn't reach their ends.
There are 2 independent parts, one for each index of `groups`. The reference program is written for one: setup_inputs(seed, part) draws one part's arguments, and reference() takes and returns one part's arrays. A program takes and returns all parts, laid end to end along the dimension named above; an argument that names none is the same for every part. Nothing has to cross between parts.
Inputs may be any that keep to these rules, and one draw needn't show every extreme that they name: `span_lists`: A list may name a span more than once; each named span is attended once.
All inputs are finite; a program needn't handle non-finite values.
Results may differ from the reference program's by a relative error of at most 0.0085.
Values may be sent and summed in bfloat16 or wider, within the bound.
No kernel may reach another device: no remote copies, remote signals or barrier semaphores. Data moves between devices by JAX's collectives and lax.ppermute only.
A program may use at most 64 MiB of HBM per device.

```python
import math
import jax
import jax.numpy as jnp
import numpy as np
from jax import lax

D = 8192
HD = 128
KVH = 4
GROUP = 8
CLEN = 512
LIST = 8
DOCS = 2
QH = 32
NEW = 2048
PLEN = 1024
NQ = 8
NCHUNK = 4


def draw_queries(key, part):
    key = jax.random.fold_in(key, 7)
    first = jax.random.fold_in(key, 0)
    return jnp.clip(jax.random.normal(first, (NQ, QH * HD), jnp.float32), -6.0, 6.0).astype(jnp.bfloat16)


def with_ends(drawn, key, smallest, high):
    place = [jax.random.randint(jax.random.fold_in(key, axis), (), 0, length) for axis, length in enumerate(drawn.shape)]
    widest = drawn.shape.index(max(drawn.shape))
    beside = place[:widest] + [(place[widest] + 1) % drawn.shape[widest]] + place[widest + 1:]
    return drawn.at[tuple(place)].set(smallest).at[tuple(beside)].set(high)


def levels(own_key, dims, cuts, smallest, top_value):
    def one(axis_at, shards_of):
        heights = jax.random.uniform(jax.random.fold_in(jax.random.fold_in(own_key, 6), axis_at), (shards_of,), jnp.float32, smallest / len(cuts), top_value / len(cuts))
        return jnp.repeat(jnp.exp(heights), dims[axis_at] // shards_of).reshape((-1,) + (1,) * (len(dims) - axis_at - 1))

    gain = one(*cuts[0])
    for cut in cuts[1:]:
        gain = gain * one(*cut)
    return gain


def cumulative_ranks(amount, skew):
    weights = [(1 << 20) // math.isqrt(grade ** skew) + 1 for grade in range(1, amount + 1)]
    scale = 1 + sum(weights) // (1 << 30)
    return np.cumsum(np.array([max(1, weight // scale) for weight in weights]))


def ranked(key, extent, number_of, slope):
    grid = cumulative_ranks(number_of, slope)
    lot = jax.random.randint(jax.random.fold_in(key, 1), extent, 0, int(grid[number_of - 1]))
    standing = jnp.searchsorted(jnp.asarray(grid, jnp.int32), lot, side="right")
    return jax.random.permutation(jax.random.fold_in(key, 2), number_of)[standing].astype(jnp.int32)


def centred(key, extent, scale, bound, shards=(), held_as=jnp.bfloat16):
    level = levels(key, extent, shards, -0.22, 0.18) if shards else 1.0
    drawn = jax.random.normal(key, extent, jnp.float32) * scale * level
    return jnp.minimum(jnp.maximum(drawn, -bound), bound).astype(held_as)


def setup_inputs(seed: int = 0, part: int = 0) -> dict:
    key_of = jax.random.split(jax.random.key(seed), 8)
    own_keys = jax.random.split(jax.random.fold_in(key_of[7], part), 8)
    return {
        "new_tokens": centred(own_keys[0], (NEW, D), 1.0, 6.0, ((0, 8),)),
        "kv_weight": centred(key_of[1], (D, KVH * 2 * HD), D ** -0.5, 0.0625, ((0, 8), (1, 2))),
        "prefix_cache": centred(own_keys[2], (DOCS, PLEN, KVH * 2 * HD), 1.0, 6.0, ((1, 8), (2, 2))),
        "queries": draw_queries(jax.random.fold_in(jax.random.fold_in(key_of[7], part), 71), part),
        "doc_of_question": with_ends(jax.random.randint(own_keys[4], (NQ,), 0, DOCS), jax.random.fold_in(own_keys[4], 1), 0, DOCS - 1).astype(jnp.int32),
        "span_lists": with_ends(ranked(own_keys[5], (NQ, LIST), NCHUNK, 2), jax.random.fold_in(own_keys[5], 3), 0, NCHUNK - 1).astype(jnp.int32),
        "span_slot": jax.random.permutation(own_keys[6], NCHUNK).astype(jnp.int32),
    }


def reference(new_tokens, kv_weight, prefix_cache, queries, doc_of_question, span_lists, span_slot):
    new_cache = jnp.dot(new_tokens, kv_weight, preferred_element_type=jnp.float32).astype(jnp.bfloat16)
    stacked = jnp.concatenate([prefix_cache.reshape(DOCS * PLEN, KVH, 2, HD), new_cache.reshape(NEW, KVH, 2, HD)], 0)
    keys_all = stacked[:, :, 0].astype(jnp.float32)
    values_all = stacked[:, :, 1].astype(jnp.float32)
    key_doc = jnp.concatenate([jnp.arange(DOCS * PLEN).astype(jnp.int32) // PLEN, jnp.full((NEW,), -1, jnp.int32)])
    key_slot = jnp.concatenate([jnp.full((DOCS * PLEN,), -1, jnp.int32), jnp.arange(NEW).astype(jnp.int32) // CLEN])
    wanted = span_slot[span_lists].astype(jnp.int32)
    asked = queries.reshape(NQ // 8, 8, KVH, GROUP, HD)
    docs = doc_of_question.reshape(NQ // 8, 8)
    slots = wanted.reshape(NQ // 8, 8, LIST)
    scale = 1.0 / (HD ** 0.5)

    def block(items):
        query_block, doc_block, slot_block = items
        visible = (doc_block[:, None] == key_doc[None, :]) | jnp.any(slot_block[:, :, None] == key_slot[None, None, :], axis=1)
        scores = jnp.einsum("qgjd,kgd->qgjk", query_block.astype(jnp.float32), keys_all) * scale
        scores = jnp.where(visible[:, None, None, :], scores, -jnp.inf)
        peak = jnp.max(scores, axis=-1)
        weights = jnp.exp(scores - peak[..., None])
        total = jnp.sum(weights, axis=-1)
        mixed = jnp.einsum("qgjk,kgd->qgjd", weights.astype(jnp.bfloat16).astype(jnp.float32), values_all)
        return (mixed / total[..., None]).astype(jnp.bfloat16).reshape(8, QH * HD)

    attended = lax.map(block, (asked, docs, slots)).reshape(NQ, QH * HD)
    return new_cache, attended
```

```python
import functools

import jax
import jax.numpy as jnp
from jax import lax
from jax.experimental import pallas as pl
from jax.experimental.pallas import tpu as pltpu
from jax.sharding import Mesh
from jax.sharding import PartitionSpec as P

HD = 128
GROUP = 8
CLEN = 512
DOCS = 2
FLIPS = ((0, 0), (1, 0), (0, 1), (1, 1))
SWAP = [(0, 1), (1, 0)]


def flip_pairs(dx, dy):
    return [((y * 2 + x), ((y ^ dy) * 2 + (x ^ dx))) for y in range(2) for x in range(2)]


def plane_permute(a, flip):
    dx, dy = flip
    if dy == 0:
        return lax.ppermute(a, "x", SWAP)
    if dx == 0:
        return lax.ppermute(a, "y", SWAP)
    return lax.ppermute(a, ("y", "x"), flip_pairs(dx, dy))


def dot32(a, b):
    return jnp.dot(a, b, preferred_element_type=jnp.float32)


def line_gather(w, z):
    pair = [(0, 1), (1, 0), (2, 3), (3, 2)]
    middle = [(1, 2), (2, 1)]
    outward = [(1, 0), (2, 3)]
    near = lax.ppermute(w, "z", pair)
    across = lax.ppermute(w, "z", middle)
    across_next = lax.ppermute(near, "z", middle)
    out = lax.ppermute(across, "z", outward)
    out_next = lax.ppermute(across_next, "z", outward)
    edge = (z == 0) | (z == 3)
    low = z < 2
    third = jnp.where(edge, out, across)
    fourth = jnp.where(edge, out_next, across_next)
    return [
        (z, w),
        (z ^ 1, near),
        (jnp.where(low, 2, 1), third),
        (jnp.where(low, 3, 0), fourth),
    ]


def project(tokens, weight):
    x, y, z, c = (lax.axis_index(a) for a in ("x", "y", "z", "c"))
    rows = tokens.shape[0]
    half = weight.shape[0] // 2
    nz, hz = 4, 2

    mine = lax.dynamic_slice_in_dim(weight, y * half, half, 0)
    blocks = line_gather(mine, z)

    view = tokens.reshape(rows, 2, hz, 2, 2, half)

    def piece(core, px, py):
        t = lax.dynamic_slice(view, (0, core, 0, px, py, 0), (rows, 1, hz, 1, 1, half))
        return jnp.transpose(t.reshape(rows, hz, half), (1, 0, 2))

    first = [piece(c, x, y)]
    second = [piece(1 - c, x, y)]
    for flip in FLIPS[1:]:
        got = plane_permute(piece(c, x ^ flip[0], y ^ flip[1]), flip)
        first.append(got)
        second.append(lax.ppermute(got, "c", SWAP))
    tall = jnp.concatenate([jnp.concatenate(first, 1), jnp.concatenate(second, 1)], 0)

    acc = None
    for source, block in blocks:
        at = lax.rem(source + c * hz, nz)
        t = lax.dynamic_index_in_dim(tall, at, 0, False)
        term = dot32(t, block)
        acc = term if acc is None else acc + term
    total = acc[:rows]
    for i, flip in enumerate(FLIPS):
        if i:
            total = total + plane_permute(acc[i * rows : (i + 1) * rows], flip)
    return total.astype(jnp.bfloat16)


def attend_kernel(q_ref, bias_ref, pre_ref, new_ref, out_ref):
    heads = q_ref.shape[0]
    rows = q_ref.shape[1]
    docs, pref_rows = pre_ref.shape[0], pre_ref.shape[1]
    lane = lax.broadcasted_iota(jnp.int32, (rows, HD), 1)
    contract = (((1,), (1,)), ((), ()))
    for g in range(heads):
        key = slice(2 * g * HD, (2 * g + 1) * HD)
        val = slice((2 * g + 1) * HD, (2 * g + 2) * HD)
        q = q_ref[g]
        parts = [(pre_ref[d, :, key], pre_ref[d, :, val]) for d in range(docs)]
        parts.append((new_ref[:, key], new_ref[:, val]))
        scores = []
        at = 0
        for k, _ in parts:
            s = lax.dot_general(q, k, contract, preferred_element_type=jnp.float32)
            s = s * (1.0 / HD**0.5) + bias_ref[:, at : at + k.shape[0]]
            scores.append(s)
            at += k.shape[0]
        peak = functools.reduce(jnp.maximum, [jnp.max(s, axis=1, keepdims=True) for s in scores])
        total = jnp.zeros((rows, 1), jnp.float32)
        mixed = jnp.zeros((rows, HD), jnp.float32)
        for s, (_, v) in zip(scores, parts):
            e = jnp.exp(s - peak)
            total = total + jnp.sum(e, axis=1, keepdims=True)
            mixed = mixed + jnp.dot(e.astype(jnp.bfloat16), v, preferred_element_type=jnp.float32)
        stat = jnp.where(lane < HD // 2, peak, total)
        n_quest = rows // GROUP
        out_ref[:, 0, g] = mixed.reshape(n_quest, GROUP, HD)
        out_ref[:, 1, g] = stat.reshape(n_quest, GROUP, HD)


def finish_kernel(n_dev, part_ref, out_ref):
    own = part_ref.shape[0] // n_dev
    heads = part_ref.shape[2]
    for r in range(own):
        for g in range(heads):
            peaks = [part_ref[d * own + r, 1, g, :, 0:1] for d in range(n_dev)]
            top = functools.reduce(jnp.maximum, peaks)
            total = jnp.zeros((GROUP, 1), jnp.float32)
            mixed = jnp.zeros((GROUP, HD), jnp.float32)
            for d in range(n_dev):
                scale = jnp.exp(peaks[d] - top)
                total = total + scale * part_ref[d * own + r, 1, g, :, HD // 2 : HD // 2 + 1]
                mixed = mixed + scale * part_ref[d * own + r, 0, g]
            done = (mixed / total).astype(jnp.bfloat16)
            for j in range(GROUP):
                at = (g * GROUP + j) * HD
                out_ref[r : r + 1, at : at + HD] = done[j : j + 1]


def shards(tokens, weight, prefix, queries, doc, lists, slots):
    nz = lax.axis_size("z")
    x, z = lax.axis_index("x"), lax.axis_index("z")
    rows = tokens.shape[0]
    heads = weight.shape[1] // (2 * HD)
    own_q = queries.shape[0]

    if nz == 4:
        new_cache = project(tokens, weight)
    else:
        new_cache = dot32(tokens, lax.all_gather(weight, ("z", "x"), axis=0, tiled=True)).astype(jnp.bfloat16)

    pair_q = jnp.concatenate([queries, lax.ppermute(queries, "x", SWAP)], 0)
    swapped = jnp.concatenate([pair_q[own_q:], pair_q[:own_q]], 0)
    pair_q = jnp.where(x == 0, pair_q, swapped)
    if nz == 4:
        near_q = lax.ppermute(pair_q, "z", [(0, 1), (1, 0), (2, 3), (3, 2)])
        low_q = jnp.where(z % 2 == 0, pair_q, near_q)
        high_q = jnp.where(z % 2 == 0, near_q, pair_q)
        half_q = jnp.concatenate([low_q, high_q], 0)
        far_q = lax.ppermute(half_q, "z", [(0, 2), (2, 0), (1, 3), (3, 1)])
        asked = jnp.concatenate([jnp.where(z < 2, half_q, far_q), jnp.where(z < 2, far_q, half_q)], 0)
    else:
        asked = lax.all_gather(pair_q, "z", axis=0, tiled=True)
    n_quest = asked.shape[0]
    asked = jnp.transpose(asked.reshape(n_quest, heads, GROUP, HD), (1, 0, 2, 3))
    asked = asked.reshape(heads, n_quest * GROUP, HD)

    pref_rows = prefix.shape[1]
    row_slot = ((z * 2 + x) * rows + jnp.arange(rows, dtype=jnp.int32)) // CLEN
    key_doc = jnp.concatenate(
        [jnp.arange(DOCS * pref_rows, dtype=jnp.int32) // pref_rows, jnp.full((rows,), -1, jnp.int32)]
    )
    key_slot = jnp.concatenate([jnp.full((DOCS * pref_rows,), -1, jnp.int32), row_slot])
    wanted = slots[lists]
    visible = (doc[:, None] == key_doc[None, :]) | jnp.any(
        wanted[:, :, None] == key_slot[None, None, :], axis=1
    )
    bias = jnp.where(visible, 0.0, -jnp.inf).astype(jnp.float32)
    bias = jnp.repeat(bias, GROUP, axis=0)

    part = pl.pallas_call(
        attend_kernel,
        out_shape=jax.ShapeDtypeStruct((n_quest, 2, heads, GROUP, HD), jnp.float32),
        compiler_params=pltpu.CompilerParams(vmem_limit_bytes=48 * 2**20),
    )(asked, bias, prefix, new_cache)
    part = lax.all_to_all(part, ("z", "x"), 0, 0, tiled=True)
    attended = pl.pallas_call(
        functools.partial(finish_kernel, 2 * nz),
        out_shape=jax.ShapeDtypeStruct((own_q, heads * GROUP * HD), jnp.bfloat16),
        compiler_params=pltpu.CompilerParams(vmem_limit_bytes=48 * 2**20),
    )(part)
    return new_cache, attended


def solution(mesh):
    groups, wide, narrow = (mesh.shape[a] for a in ("groups", "wide", "narrow"))
    split = Mesh(mesh.devices.reshape(groups, wide // 2, 2, narrow), ("y", "z", "x", "c"))
    row = ("y", "z", "x")
    placed = (
        P(row, None),
        P(("z", "x"), "c"),
        P(None, row, "c"),
        P(row, "c"),
        P("y"),
        P("y", None),
        P("y"),
    )
    return jax.shard_map(
        shards,
        mesh=split,
        in_specs=placed,
        out_specs=(P(row, "c"), P(row, "c")),
        check_vma=False,
    )
```

```python
import functools

import jax
import jax.numpy as jnp
from jax import lax
from jax.experimental import pallas as pl
from jax.experimental.pallas import tpu as pltpu
from jax.sharding import Mesh
from jax.sharding import PartitionSpec as P

HD = 128
GROUP = 8
CLEN = 512
DOCS = 2
FLIPS = ((0, 0), (1, 0), (0, 1), (1, 1))
SWAP = [(0, 1), (1, 0)]
ALL = pltpu.CompilerParams(vmem_limit_bytes=60 * 2**20)
ROOM = pltpu.CompilerParams(vmem_limit_bytes=16 * 2**20)


def flip_pairs(dx, dy):
    return [((y * 2 + x), ((y ^ dy) * 2 + (x ^ dx))) for y in range(2) for x in range(2)]


def plane_permute(a, flip):
    dx, dy = flip
    if dy == 0:
        return lax.ppermute(a, "x", SWAP)
    if dx == 0:
        return lax.ppermute(a, "y", SWAP)
    return lax.ppermute(a, ("y", "x"), flip_pairs(dx, dy))


def dot32(a, b):
    return jnp.dot(a, b, preferred_element_type=jnp.float32)


def order_of(z):
    low = z < 2
    return [z, z ^ 1, jnp.where(low, 2, 1), jnp.where(low, 3, 0)]


def add_block(core, firsts, seconds, block):
    width = block.shape[0] // 2
    top, bottom = block[:width], block[width:]
    near = jnp.where(core == 0, top, bottom)
    far = jnp.where(core == 0, bottom, top)
    return [dot32(f, near) + dot32(s, far) for f, s in zip(firsts, seconds)]


def carve_kernel(flips, place_ref, tokens, *refs):
    *piece_refs, sems = refs
    width = piece_refs[0].shape[1] // 4
    order = [place_ref[i] for i in range(4)]
    core, x, y = place_ref[4], place_ref[6], place_ref[7]
    copies = []
    for n, (ref, (dx, dy, dc)) in enumerate(zip(piece_refs, flips)):
        for i, s in enumerate(order):
            at = (((s * 2 + (x ^ dx)) * 2 + (y ^ dy)) * 2 + (core ^ dc)) * width
            copies.append(
                pltpu.make_async_copy(
                    tokens.at[:, pl.ds(pl.multiple_of(at, width), width)],
                    ref.at[:, pl.ds(i * width, width)],
                    sems.at[n * 4 + i],
                )
            )
    for copy in copies:
        copy.start()
    for copy in copies:
        copy.wait()


def add_up(place_ref, firsts, seconds, blocks, half, start, sums):
    width = half // 2
    for index, block in enumerate(blocks, start):
        cut = slice(index * width, (index + 1) * width)
        terms = add_block(place_ref[4], [f[:, cut] for f in firsts], [s[:, cut] for s in seconds], block[:half])
        sums = [term if s is None else s + term for s, term in zip(sums, terms)]
    return sums


def early_kernel(half, place_ref, *refs):
    firsts, seconds, (own, near), acc_ref = refs[:3], refs[3:6], refs[6:8], refs[8]
    for b, s in enumerate(add_up(place_ref, firsts, seconds, [own, near], half, 0, [None] * 3)):
        acc_ref[b] = s


def late_blocks(place_ref, across, out, across_next, out_next):
    edge = place_ref[5] == 1
    return [jnp.where(edge, out[...], across[...]), jnp.where(edge, out_next[...], across_next[...])]


def late_kernel(half, place_ref, *refs):
    firsts, seconds, acc_ref, keep_ref, send_refs = refs[:3], refs[3:6], refs[6], refs[11], refs[12:]
    blocks = late_blocks(place_ref, *refs[7:11])
    sums = add_up(place_ref, firsts, seconds, blocks, half, 2, [acc_ref[b] for b in range(3)])
    keep_ref[...] = sums[0]
    for send, part in zip(send_refs, sums[1:]):
        pack(part, send)


def last_kernel(half, place_ref, first, second, own, near, across, out, across_next, out_next, send_ref, line_ref):
    blocks = [own[...], near[...], *late_blocks(place_ref, across, out, across_next, out_next)]
    for i, block in enumerate(blocks):
        line_ref[place_ref[i]] = block[half:]
    pack(add_up(place_ref, [first], [second], blocks, half, 0, [None])[0], send_ref)


def pack(part, ref):
    for g in range(part.shape[1] // (2 * HD)):
        key = part[:, 2 * g * HD : (2 * g + 1) * HD]
        high = key.astype(jnp.bfloat16)
        at = 3 * g * HD
        ref[:, at : at + HD] = high
        ref[:, at + HD : at + 2 * HD] = (key - high.astype(jnp.float32)).astype(jnp.bfloat16)
        ref[:, at + 2 * HD : at + 3 * HD] = part[:, (2 * g + 1) * HD : (2 * g + 2) * HD].astype(jnp.bfloat16)


def unpack(ref, g):
    at = 3 * g * HD
    high, low, value = (ref[:, at + i * HD : at + (i + 1) * HD].astype(jnp.float32) for i in range(3))
    return high + low, value


def project(tokens, weight, queries):
    x, y, z, c = (lax.axis_index(a) for a in ("x", "y", "z", "c"))
    rows = tokens.shape[0]
    columns = weight.shape[1]
    half = weight.shape[0] // 2
    nz = 4
    edge = (z == 0) | (z == 3)
    place = jnp.stack([*order_of(z), c, edge, x, y]).astype(jnp.int32)
    fence = lax.optimization_barrier
    own_q, q_width = queries.shape
    q_rows = own_q * q_width // columns
    q_room = q_rows + -q_rows % 16
    smem = pl.BlockSpec(memory_space=pltpu.SMEM)
    vmem = pl.BlockSpec(memory_space=pltpu.VMEM)
    hbm = pl.BlockSpec(memory_space=pltpu.HBM)

    flips = [(dx, dy, 0) for dx, dy in FLIPS[1:]] + [(0, 0, 0), (0, 0, 1)]
    piece = jax.ShapeDtypeStruct((rows, 2 * half), tokens.dtype)
    own = jnp.concatenate(
        [
            lax.dynamic_slice_in_dim(weight, y * half, half, 0),
            jnp.pad(queries.reshape(q_rows, columns), ((0, q_room - q_rows), (0, 0))),
        ],
        0,
    )
    own, tokens = fence((own, tokens))
    piece_x, piece_y, piece_d, kept, kept_other = pl.pallas_call(
        functools.partial(carve_kernel, flips),
        in_specs=[smem, hbm],
        out_specs=[vmem] * 5,
        out_shape=[piece] * 5,
        scratch_shapes=[pltpu.SemaphoreType.DMA((20,))],
        compiler_params=ALL,
    )(place, tokens)
    middle, outward = [(1, 2), (2, 1)], [(1, 0), (2, 3)]
    near = lax.ppermute(own, "z", [(0, 1), (1, 0), (2, 3), (3, 2)])
    across = lax.ppermute(own, "z", middle)
    across_next = lax.ppermute(near, "z", middle)
    out = lax.ppermute(across, "z", outward)
    across_then, _ = fence((across_next, out))
    out_next = lax.ppermute(across_then, "z", outward)
    tok_x = plane_permute(piece_x, FLIPS[1])
    tok_y = plane_permute(piece_y, FLIPS[2])
    tok_x, tok_y, piece_d = fence((tok_x, tok_y, piece_d))
    tok_d = plane_permute(piece_d, FLIPS[3])
    other_x, other_y, other_d = (lax.ppermute(t, "c", SWAP) for t in (tok_x, tok_y, tok_d))
    firsts, seconds = [kept, tok_x, tok_y], [kept_other, other_x, other_y]

    line = jax.ShapeDtypeStruct((nz, q_room, columns), queries.dtype)
    free = pl.BlockSpec()
    acc = pl.pallas_call(
        functools.partial(early_kernel, half),
        in_specs=[smem] + [free] * 8,
        out_specs=free,
        out_shape=jax.ShapeDtypeStruct((3, rows, columns), jnp.float32),
        compiler_params=ROOM,
    )(place, *firsts, *seconds, own, near)
    keep = jax.ShapeDtypeStruct((rows, columns), jnp.float32)
    send = jax.ShapeDtypeStruct((rows, columns // 2 * 3), jnp.bfloat16)
    arrived = (across, out, across_next, out_next)
    keep, send_x, send_y = pl.pallas_call(
        functools.partial(late_kernel, half),
        in_specs=[smem] + [free] * 11,
        out_specs=[free] * 3,
        out_shape=[keep, send, send],
        cost_estimate=pl.CostEstimate(flops=10**10, bytes_accessed=10**7, transcendentals=0),
        compiler_params=ROOM,
    )(place, *firsts, *seconds, acc, *arrived)
    send_d, line_q = pl.pallas_call(
        functools.partial(last_kernel, half),
        in_specs=[smem] + [free] * 8,
        out_specs=[free] * 2,
        out_shape=[send, line],
        compiler_params=ROOM,
    )(place, tok_d, other_d, own, near, *arrived)
    parts = [keep] + [plane_permute(p, flip) for p, flip in zip((send_x, send_y, send_d), FLIPS[1:])]

    line_q = line_q[:, :q_rows]
    other_q = lax.ppermute(line_q, "x", SWAP)
    low_q = jnp.where(x == 0, line_q, other_q).reshape(nz, own_q, q_width)
    high_q = jnp.where(x == 0, other_q, line_q).reshape(nz, own_q, q_width)
    asked = jnp.stack([low_q, high_q], 1).reshape(nz * 2 * own_q, q_width)
    return parts, asked


def attend_kernel(q_ref, bias_ref, pre_ref, *refs):
    keep_ref, *got_refs, new_ref, out_ref = refs
    for g in range(q_ref.shape[0]):
        cut = [slice((2 * g + i) * HD, (2 * g + i + 1) * HD) for i in range(2)]
        sums = [keep_ref[:, at] for at in cut]
        for got in got_refs:
            sums = [s + more for s, more in zip(sums, unpack(got, g))]
        for at, s in zip(cut, sums):
            new_ref[:, at] = s.astype(jnp.bfloat16)
    heads = q_ref.shape[0]
    rows = q_ref.shape[1]
    docs, pref_rows = pre_ref.shape[0], pre_ref.shape[1]
    lane = lax.broadcasted_iota(jnp.int32, (rows, HD), 1)
    contract = (((1,), (1,)), ((), ()))
    stat = jnp.zeros((rows, HD), jnp.float32)
    for g in range(heads):
        key = slice(2 * g * HD, (2 * g + 1) * HD)
        val = slice((2 * g + 1) * HD, (2 * g + 2) * HD)
        q = q_ref[g]
        parts = [(pre_ref[d, :, key], pre_ref[d, :, val]) for d in range(docs)]
        parts.append((new_ref[:, key], new_ref[:, val]))
        scores = []
        at = 0
        for k, _ in parts:
            s = lax.dot_general(q, k, contract, preferred_element_type=jnp.float32)
            s = s * (1.0 / HD**0.5) + bias_ref[:, at : at + k.shape[0]]
            scores.append(s)
            at += k.shape[0]
        peak = functools.reduce(jnp.maximum, [jnp.max(s, axis=1, keepdims=True) for s in scores])
        total = jnp.zeros((rows, 1), jnp.float32)
        mixed = jnp.zeros((rows, HD), jnp.float32)
        for s, (_, v) in zip(scores, parts):
            e = jnp.exp(s - peak)
            total = total + jnp.sum(e, axis=1, keepdims=True)
            mixed = mixed + jnp.dot(e.astype(jnp.bfloat16), v, preferred_element_type=jnp.float32)
        n_quest = rows // GROUP
        out_ref[:, g] = mixed.reshape(n_quest, GROUP, HD)
        stat = jnp.where(lane == 2 * g, peak, jnp.where(lane == 2 * g + 1, total, stat))
    out_ref[:, heads] = stat.reshape(n_quest, GROUP, HD)


def finish_kernel(n_dev, part_ref, out_ref):
    own = part_ref.shape[0] // n_dev
    heads = part_ref.shape[1] - 1
    for r in range(own):
        for g in range(heads):
            peaks = [part_ref[d * own + r, heads, :, 2 * g : 2 * g + 1] for d in range(n_dev)]
            top = functools.reduce(jnp.maximum, peaks)
            total = jnp.zeros((GROUP, 1), jnp.float32)
            mixed = jnp.zeros((GROUP, HD), jnp.float32)
            for d in range(n_dev):
                scale = jnp.exp(peaks[d] - top)
                total = total + scale * part_ref[d * own + r, heads, :, 2 * g + 1 : 2 * g + 2]
                mixed = mixed + scale * part_ref[d * own + r, g]
            done = (mixed / total).astype(jnp.bfloat16)
            for j in range(GROUP):
                at = (g * GROUP + j) * HD
                out_ref[r : r + 1, at : at + HD] = done[j : j + 1]


def shards(tokens, weight, prefix, queries, doc, lists, slots):
    nz = lax.axis_size("z")
    x, z = lax.axis_index("x"), lax.axis_index("z")
    rows = tokens.shape[0]
    heads = weight.shape[1] // (2 * HD)
    own_q = queries.shape[0]

    if nz == 4:
        parts, asked = project(tokens, weight, queries)
    else:
        parts = [dot32(tokens, lax.all_gather(weight, ("z", "x"), axis=0, tiled=True))]
        asked = lax.all_gather(queries, ("z", "x"), axis=0, tiled=True)
    n_quest = asked.shape[0]
    asked = jnp.transpose(asked.reshape(n_quest, heads, GROUP, HD), (1, 0, 2, 3))
    asked = asked.reshape(heads, n_quest * GROUP, HD)

    pref_rows = prefix.shape[1]
    row_slot = ((z * 2 + x) * rows + jnp.arange(rows, dtype=jnp.int32)) // CLEN
    key_doc = jnp.concatenate(
        [jnp.arange(DOCS * pref_rows, dtype=jnp.int32) // pref_rows, jnp.full((rows,), -1, jnp.int32)]
    )
    key_slot = jnp.concatenate([jnp.full((DOCS * pref_rows,), -1, jnp.int32), row_slot])
    wanted = slots[lists]
    visible = (doc[:, None] == key_doc[None, :]) | jnp.any(
        wanted[:, :, None] == key_slot[None, None, :], axis=1
    )
    bias = jnp.where(visible, 0.0, -jnp.inf).astype(jnp.float32)
    bias = jnp.repeat(bias, GROUP, axis=0)

    new_cache, part = pl.pallas_call(
        attend_kernel,
        out_shape=(
            jax.ShapeDtypeStruct(parts[0].shape, jnp.bfloat16),
            jax.ShapeDtypeStruct((n_quest, heads + 1, GROUP, HD), jnp.float32),
        ),
        compiler_params=ROOM,
    )(asked, bias, prefix, *parts)
    part = lax.all_to_all(part, ("z", "x"), 0, 0, tiled=True)
    attended = pl.pallas_call(
        functools.partial(finish_kernel, 2 * nz),
        out_shape=jax.ShapeDtypeStruct((own_q, heads * GROUP * HD), jnp.bfloat16),
        compiler_params=ROOM,
    )(part)
    return new_cache, attended


def solution(mesh):
    groups, wide, narrow = (mesh.shape[a] for a in ("groups", "wide", "narrow"))
    split = Mesh(mesh.devices.reshape(groups, wide // 2, 2, narrow), ("y", "z", "x", "c"))
    row = ("y", "z", "x")
    placed = (
        P(row, None),
        P(("z", "x"), "c"),
        P(None, row, "c"),
        P(row, "c"),
        P("y"),
        P("y", None),
        P("y"),
    )
    return jax.shard_map(
        shards,
        mesh=split,
        in_specs=placed,
        out_specs=(P(row, "c"), P(row, "c")),
        check_vma=False,
    )
```

```python
import functools

import jax
import jax.numpy as jnp
from jax import lax
from jax.experimental import pallas as pl
from jax.experimental.pallas import tpu as pltpu
from jax.sharding import Mesh
from jax.sharding import PartitionSpec as P

HD = 128
GROUP = 8
CLEN = 512
DOCS = 2
SWAP = [(0, 1), (1, 0)]
ALL = pltpu.CompilerParams(vmem_limit_bytes=60 * 2**20)
ROOM = pltpu.CompilerParams(vmem_limit_bytes=16 * 2**20)


def dot32(a, b):
    return jnp.dot(a, b, preferred_element_type=jnp.float32)


def order_of(z):
    low = z < 2
    return [z, z ^ 1, jnp.where(low, 2, 1), jnp.where(low, 3, 0)]


def carve_kernel(place_ref, tokens, *refs):
    piece_refs, sems = refs[:3], refs[3]
    width = piece_refs[0].shape[1] // 4
    core, x = place_ref[4], place_ref[6]
    copies = []
    for n, (ref, (dx, dc)) in enumerate(zip(piece_refs, ((1, 0), (0, 0), (0, 1)))):
        for i in range(4):
            at = ((place_ref[i] * 2 + (x ^ dx)) * 2 + (core ^ dc)) * width
            copies.append(
                pltpu.make_async_copy(
                    tokens.at[:, pl.ds(pl.multiple_of(at, width), width)],
                    ref.at[:, pl.ds(i * width, width)],
                    sems.at[n * 4 + i],
                )
            )
    for copy in copies:
        copy.start()
    for copy in copies:
        copy.wait()


def half_terms(place_ref, firsts, seconds, index, along_z, along_y):
    width = firsts[0].shape[1] // 4
    cut = slice(index * width, (index + 1) * width)
    same = place_ref[4] == place_ref[7]
    terms = [None] * len(firsts)
    for block, mine in ((along_z, same), (along_y, jnp.logical_not(same))):
        if block is not None:
            for b, (f, s) in enumerate(zip(firsts, seconds)):
                term = dot32(jnp.where(mine, f[:, cut], s[:, cut]), block)
                terms[b] = term if terms[b] is None else terms[b] + term
    return terms


def early_kernel(half, place_ref, *refs):
    firsts, seconds, (own, weight, near, y_near, acc_ref, weight_ref, sem) = refs[:2], refs[2:4], refs[4:]
    load = pltpu.make_async_copy(
        weight.at[pl.ds(pl.multiple_of((1 - place_ref[7]) * half, half), half)], weight_ref, sem
    )
    load.start()
    sums = half_terms(place_ref, firsts, seconds, 1, near[:half], y_near[:half])
    load.wait()
    terms = half_terms(place_ref, firsts, seconds, 0, own[:half], weight_ref[...])
    for b in range(2):
        acc_ref[b] = sums[b] + terms[b]


def middle_kernel(half, q_rows, place_ref, *refs):
    firsts, seconds = refs[:2], refs[2:4]
    old_ref, own, near, third, fourth, y_third, acc_ref, line_ref, left_ref = refs[4:]
    per = own.shape[1] // HD
    for i, block in enumerate((own, near, third, fourth)):
        for r in range(q_rows):
            for h in range(per):
                at = slice(h * HD, (h + 1) * HD)
                line_ref[place_ref[i], r * per + h : r * per + h + 1] = block[half + r : half + r + 1, at]
    sums = half_terms(place_ref, firsts, seconds, 2, third[:half], y_third[:half])
    terms = half_terms(place_ref, firsts, seconds, 3, fourth[:half], None)
    width = left_ref.shape[2]
    cut = slice(3 * width, 4 * width)
    other = place_ref[4] != place_ref[7]
    for b in range(2):
        acc_ref[b] = old_ref[b] + sums[b] + terms[b]
        left_ref[b] = jnp.where(other, firsts[b][:, cut], seconds[b][:, cut])


def late_kernel(half, left_ref, acc_ref, block_ref, keep_out, send_out, keep_ref, send_ref, sems):
    block = block_ref[:half]
    pack(acc_ref[1] + dot32(left_ref[1], block), send_ref)
    copies = [
        pltpu.make_async_copy(send_ref, send_out, sems.at[0]),
        pltpu.make_async_copy(keep_ref, keep_out, sems.at[1]),
    ]
    copies[0].start()
    keep_ref[...] = acc_ref[0] + dot32(left_ref[0], block)
    copies[1].start()
    for copy in copies:
        copy.wait()


def pack(part, ref):
    for g in range(part.shape[1] // (2 * HD)):
        key = part[:, 2 * g * HD : (2 * g + 1) * HD]
        high = key.astype(jnp.bfloat16)
        at = 3 * g * HD
        ref[:, at : at + HD] = high
        ref[:, at + HD : at + 2 * HD] = (key - high.astype(jnp.float32)).astype(jnp.bfloat16)
        ref[:, at + 2 * HD : at + 3 * HD] = part[:, (2 * g + 1) * HD : (2 * g + 2) * HD].astype(jnp.bfloat16)


def unpack(ref, g):
    at = 3 * g * HD
    high, low, value = (ref[:, at + i * HD : at + (i + 1) * HD].astype(jnp.float32) for i in range(3))
    return high + low, value


def project(tokens, weight, queries):
    x, y, z, c = (lax.axis_index(a) for a in ("x", "y", "z", "c"))
    rows = tokens.shape[0]
    columns = weight.shape[1]
    half = weight.shape[0] // 2
    nz = 4
    edge = (z == 0) | (z == 3)
    place = jnp.stack([*order_of(z), c, edge, x, y]).astype(jnp.int32)
    fence = lax.optimization_barrier
    own_q, q_width = queries.shape
    q_rows = own_q * q_width // columns
    q_room = q_rows + -q_rows % 16
    smem = pl.BlockSpec(memory_space=pltpu.SMEM)
    vmem = pl.BlockSpec(memory_space=pltpu.VMEM)
    hbm = pl.BlockSpec(memory_space=pltpu.HBM)
    anywhere = pl.BlockSpec(memory_space=pl.ANY)
    free = pl.BlockSpec()

    own = jnp.concatenate(
        [
            lax.dynamic_slice_in_dim(weight, y * half, half, 0),
            jnp.pad(queries.reshape(q_rows, columns), ((0, q_room - q_rows), (0, 0))),
        ],
        0,
    )
    own, tokens = fence((own, tokens))
    piece = jax.ShapeDtypeStruct((rows, 4 * half), tokens.dtype)
    piece_x, kept, kept_other = pl.pallas_call(
        carve_kernel,
        in_specs=[smem, hbm],
        out_specs=[vmem] * 3,
        out_shape=[piece] * 3,
        scratch_shapes=[pltpu.SemaphoreType.DMA((12,))],
        compiler_params=ALL,
    )(place, tokens)
    middle, outward = [(1, 2), (2, 1)], [(1, 0), (2, 3)]
    near = lax.ppermute(own, "z", [(0, 1), (1, 0), (2, 3), (3, 2)])
    across = lax.ppermute(own, "z", middle)
    tok = lax.ppermute(piece_x, "x", SWAP)

    across_next = lax.ppermute(near, "z", middle)
    out = lax.ppermute(across, "z", outward)
    y_near = lax.ppermute(near, "y", SWAP)

    across_next, out, y_near = fence((across_next, out, y_near))
    out_next = lax.ppermute(across_next, "z", outward)
    third = jnp.where(edge, out, across)
    y_third = lax.ppermute(third, "y", SWAP)

    out_next, y_third = fence((out_next, y_third))
    fourth = jnp.where(edge, out_next, across_next)
    y_fourth = lax.ppermute(fourth, "y", SWAP)
    other = lax.ppermute(tok, "c", SWAP)
    sides = (kept, tok, kept_other, other)

    acc_shape = jax.ShapeDtypeStruct((2, rows, columns), jnp.float32)
    acc = pl.pallas_call(
        functools.partial(early_kernel, half),
        in_specs=[smem] + [free] * 5 + [anywhere] + [free] * 2,
        out_specs=free,
        out_shape=acc_shape,
        scratch_shapes=[pltpu.VMEM((half, columns), weight.dtype), pltpu.SemaphoreType.DMA],
        compiler_params=ROOM,
    )(place, *sides, own, weight, near, y_near)
    acc, line_q, left = pl.pallas_call(
        functools.partial(middle_kernel, half, q_rows),
        in_specs=[smem] + [free] * 10,
        out_specs=[free] * 3,
        out_shape=[
            acc_shape,
            jax.ShapeDtypeStruct((nz, q_rows * columns // HD, HD), queries.dtype),
            jax.ShapeDtypeStruct((2, rows, half), tokens.dtype),
        ],
        compiler_params=ROOM,
    )(place, *sides, acc, own, near, third, fourth, y_third)
    keep = ((rows, columns), jnp.float32)
    send = ((rows, columns // 2 * 3), jnp.bfloat16)
    keep_here, send_x = pl.pallas_call(
        functools.partial(late_kernel, half),
        in_specs=[free] * 3,
        out_specs=[hbm] * 2,
        out_shape=[pltpu.HBM(*keep), pltpu.HBM(*send)],
        scratch_shapes=[pltpu.VMEM(*keep), pltpu.VMEM(*send), pltpu.SemaphoreType.DMA((2,))],
        compiler_params=ROOM,
    )(left, acc, y_fourth)
    parts = [keep_here, lax.ppermute(send_x, "x", SWAP)]

    other_q = lax.ppermute(line_q, "x", SWAP)
    asked = jnp.stack([jnp.where(x == 0, line_q, other_q), jnp.where(x == 0, other_q, line_q)], 1)
    heads = columns // (2 * HD)
    asked = asked.reshape(nz, 2, own_q, heads, GROUP, HD).transpose(3, 0, 1, 2, 4, 5)
    asked = asked.reshape(heads, nz * 2 * own_q * GROUP, HD)
    return parts, asked


def attend_kernel(q_ref, bias_ref, pre_ref, *refs):
    keep_ref, *got_refs, new_ref, out_ref = refs
    for g in range(q_ref.shape[0]):
        cut = [slice((2 * g + i) * HD, (2 * g + i + 1) * HD) for i in range(2)]
        sums = [keep_ref[:, at] for at in cut]
        for got in got_refs:
            sums = [s + more for s, more in zip(sums, unpack(got, g))]
        for at, s in zip(cut, sums):
            new_ref[:, at] = s.astype(jnp.bfloat16)
    heads = q_ref.shape[0]
    rows = q_ref.shape[1]
    docs, pref_rows = pre_ref.shape[0], pre_ref.shape[1]
    lane = lax.broadcasted_iota(jnp.int32, (rows, HD), 1)
    contract = (((1,), (1,)), ((), ()))
    stat = jnp.zeros((rows, HD), jnp.float32)
    for g in range(heads):
        key = slice(2 * g * HD, (2 * g + 1) * HD)
        val = slice((2 * g + 1) * HD, (2 * g + 2) * HD)
        q = q_ref[g]
        parts = [(pre_ref[d, :, key], pre_ref[d, :, val]) for d in range(docs)]
        parts.append((new_ref[:, key], new_ref[:, val]))
        scores = []
        at = 0
        for k, _ in parts:
            s = lax.dot_general(q, k, contract, preferred_element_type=jnp.float32)
            s = s * (1.0 / HD**0.5) + bias_ref[:, at : at + k.shape[0]]
            scores.append(s)
            at += k.shape[0]
        peak = functools.reduce(jnp.maximum, [jnp.max(s, axis=1, keepdims=True) for s in scores])
        total = jnp.zeros((rows, 1), jnp.float32)
        mixed = jnp.zeros((rows, HD), jnp.float32)
        for s, (_, v) in zip(scores, parts):
            e = jnp.exp(s - peak)
            total = total + jnp.sum(e, axis=1, keepdims=True)
            mixed = mixed + jnp.dot(e.astype(jnp.bfloat16), v, preferred_element_type=jnp.float32)
        n_quest = rows // GROUP
        out_ref[:, g] = mixed.reshape(n_quest, GROUP, HD)
        stat = jnp.where(lane == 2 * g, peak, jnp.where(lane == 2 * g + 1, total, stat))
    out_ref[:, heads] = stat.reshape(n_quest, GROUP, HD)


def finish_kernel(n_dev, part_ref, out_ref):
    own = part_ref.shape[0] // n_dev
    heads = part_ref.shape[1] - 1
    for r in range(own):
        for g in range(heads):
            peaks = [part_ref[d * own + r, heads, :, 2 * g : 2 * g + 1] for d in range(n_dev)]
            top = functools.reduce(jnp.maximum, peaks)
            total = jnp.zeros((GROUP, 1), jnp.float32)
            mixed = jnp.zeros((GROUP, HD), jnp.float32)
            for d in range(n_dev):
                scale = jnp.exp(peaks[d] - top)
                total = total + scale * part_ref[d * own + r, heads, :, 2 * g + 1 : 2 * g + 2]
                mixed = mixed + scale * part_ref[d * own + r, g]
            done = (mixed / total).astype(jnp.bfloat16)
            for j in range(GROUP):
                at = (g * GROUP + j) * HD
                out_ref[r : r + 1, at : at + HD] = done[j : j + 1]


def shards(tokens, weight, prefix, queries, doc, lists, slots):
    nz = lax.axis_size("z")
    x, z = lax.axis_index("x"), lax.axis_index("z")
    rows = tokens.shape[0]
    heads = weight.shape[1] // (2 * HD)
    own_q = queries.shape[0]

    if nz == 4:
        parts, asked = project(tokens, weight, queries)
    else:
        parts = [dot32(tokens, lax.all_gather(weight, ("z", "x"), axis=0, tiled=True))]
        asked = lax.all_gather(queries, ("z", "x"), axis=0, tiled=True)
        asked = asked.reshape(-1, heads, GROUP, HD).transpose(1, 0, 2, 3).reshape(heads, -1, HD)
    n_quest = asked.shape[1] // GROUP

    pref_rows = prefix.shape[1]
    row_slot = ((z * 2 + x) * rows + jnp.arange(rows, dtype=jnp.int32)) // CLEN
    key_doc = jnp.concatenate(
        [jnp.arange(DOCS * pref_rows, dtype=jnp.int32) // pref_rows, jnp.full((rows,), -1, jnp.int32)]
    )
    key_slot = jnp.concatenate([jnp.full((DOCS * pref_rows,), -1, jnp.int32), row_slot])
    wanted = slots[lists]
    visible = (doc[:, None] == key_doc[None, :]) | jnp.any(
        wanted[:, :, None] == key_slot[None, None, :], axis=1
    )
    bias = jnp.where(visible, 0.0, -jnp.inf).astype(jnp.float32)
    bias = jnp.repeat(bias, GROUP, axis=0)

    new_cache, part = pl.pallas_call(
        attend_kernel,
        out_shape=(
            jax.ShapeDtypeStruct(parts[0].shape, jnp.bfloat16),
            jax.ShapeDtypeStruct((n_quest, heads + 1, GROUP, HD), jnp.float32),
        ),
        compiler_params=ROOM,
    )(asked, bias, prefix, *parts)
    part = lax.all_to_all(part, ("z", "x"), 0, 0, tiled=True)
    attended = pl.pallas_call(
        functools.partial(finish_kernel, 2 * nz),
        out_shape=jax.ShapeDtypeStruct((own_q, heads * GROUP * HD), jnp.bfloat16),
        compiler_params=ROOM,
    )(part)
    return new_cache, attended


def solution(mesh):
    groups, wide, narrow = (mesh.shape[a] for a in ("groups", "wide", "narrow"))
    split = Mesh(mesh.devices.reshape(groups, wide // 2, 2, narrow), ("y", "z", "x", "c"))
    row = ("y", "z", "x")
    placed = (
        P(row, None),
        P(("z", "x"), "c"),
        P(None, row, "c"),
        P(row, "c"),
        P("y"),
        P("y", None),
        P("y"),
    )
    return jax.shard_map(
        shards,
        mesh=split,
        in_specs=placed,
        out_specs=(P(row, "c"), P(row, "c")),
        check_vma=False,
    )
```

```python
import functools

import jax
import jax.numpy as jnp
from jax import lax
from jax.experimental import pallas as pl
from jax.experimental.pallas import tpu as pltpu
from jax.sharding import Mesh
from jax.sharding import PartitionSpec as P

HD = 128
GROUP = 8
CLEN = 512
DOCS = 2
SWAP = [(0, 1), (1, 0)]
ALL = pltpu.CompilerParams(vmem_limit_bytes=60 * 2**20)
ROOM = pltpu.CompilerParams(vmem_limit_bytes=16 * 2**20)


def dot32(a, b):
    return jnp.dot(a, b, preferred_element_type=jnp.float32)


def order_of(z):
    low = z < 2
    return [z, z ^ 1, jnp.where(low, 2, 1), jnp.where(low, 3, 0)]


def carve_kernel(place_ref, tokens, *refs):
    piece_refs, sems = refs[:3], refs[3]
    width = piece_refs[0].shape[1] // 4
    core, x = place_ref[4], place_ref[6]
    copies = []
    for n, (ref, (dx, dc)) in enumerate(zip(piece_refs, ((1, 0), (0, 0), (0, 1)))):
        for i in range(4):
            at = ((place_ref[i] * 2 + (x ^ dx)) * 2 + (core ^ dc)) * width
            copies.append(
                pltpu.make_async_copy(
                    tokens.at[:, pl.ds(pl.multiple_of(at, width), width)],
                    ref.at[:, pl.ds(i * width, width)],
                    sems.at[n * 4 + i],
                )
            )
    for copy in copies:
        copy.start()
    for copy in copies:
        copy.wait()


def half_terms(place_ref, firsts, seconds, index, along_z, along_y):
    width = firsts[0].shape[1] // 4
    cut = slice(index * width, (index + 1) * width)
    same = place_ref[4] == place_ref[7]
    terms = [None] * len(firsts)
    for block, mine in ((along_z, same), (along_y, jnp.logical_not(same))):
        if block is not None:
            for b, (f, s) in enumerate(zip(firsts, seconds)):
                term = dot32(jnp.where(mine, f[:, cut], s[:, cut]), block)
                terms[b] = term if terms[b] is None else terms[b] + term
    return terms


def early_kernel(half, place_ref, *refs):
    firsts, seconds, (own, weight, near, y_near, acc_ref, weight_ref, sem) = refs[:2], refs[2:4], refs[4:]
    load = pltpu.make_async_copy(
        weight.at[pl.ds(pl.multiple_of((1 - place_ref[7]) * half, half), half)], weight_ref, sem
    )
    load.start()
    sums = half_terms(place_ref, firsts, seconds, 1, near[:half], y_near[:half])
    load.wait()
    terms = half_terms(place_ref, firsts, seconds, 0, own[:half], weight_ref[...])
    for b in range(2):
        acc_ref[b] = sums[b] + terms[b]


def middle_kernel(half, q_rows, place_ref, *refs):
    firsts, seconds = refs[:2], refs[2:4]
    old_ref, own, near, third, fourth, y_third, acc_ref, line_ref, left_ref = refs[4:]
    per = own.shape[1] // HD
    for i, block in enumerate((own, near, third, fourth)):
        for r in range(q_rows):
            for h in range(per):
                at = slice(h * HD, (h + 1) * HD)
                line_ref[place_ref[i], r * per + h : r * per + h + 1] = block[half + r : half + r + 1, at]
    sums = half_terms(place_ref, firsts, seconds, 2, third[:half], y_third[:half])
    terms = half_terms(place_ref, firsts, seconds, 3, fourth[:half], None)
    width = left_ref.shape[2]
    cut = slice(3 * width, 4 * width)
    other = place_ref[4] != place_ref[7]
    for b in range(2):
        acc_ref[b] = old_ref[b] + sums[b] + terms[b]
        left_ref[b] = jnp.where(other, firsts[b][:, cut], seconds[b][:, cut])


def mark_kernel(given_ref, mark_ref):
    mark_ref[...] = jnp.zeros_like(mark_ref)


def send_kernel(half, left_ref, acc_ref, block_ref, mark_ref, send_ref):
    pack(acc_ref[1] + dot32(left_ref[1], block_ref[:half]), send_ref)


def keep_kernel(half, left_ref, acc_ref, block_ref, keep_ref):
    keep_ref[...] = acc_ref[0] + dot32(left_ref[0], block_ref[:half])


def pack(part, ref):
    for g in range(part.shape[1] // (2 * HD)):
        key = part[:, 2 * g * HD : (2 * g + 1) * HD]
        high = key.astype(jnp.bfloat16)
        at = 3 * g * HD
        ref[:, at : at + HD] = high
        ref[:, at + HD : at + 2 * HD] = (key - high.astype(jnp.float32)).astype(jnp.bfloat16)
        ref[:, at + 2 * HD : at + 3 * HD] = part[:, (2 * g + 1) * HD : (2 * g + 2) * HD].astype(jnp.bfloat16)


def unpack(ref, g):
    at = 3 * g * HD
    high, low, value = (ref[:, at + i * HD : at + (i + 1) * HD].astype(jnp.float32) for i in range(3))
    return high + low, value


def project(tokens, weight, queries):
    x, y, z, c = (lax.axis_index(a) for a in ("x", "y", "z", "c"))
    rows = tokens.shape[0]
    columns = weight.shape[1]
    half = weight.shape[0] // 2
    nz = 4
    edge = (z == 0) | (z == 3)
    place = jnp.stack([*order_of(z), c, edge, x, y]).astype(jnp.int32)
    fence = lax.optimization_barrier
    own_q, q_width = queries.shape
    q_rows = own_q * q_width // columns
    q_room = q_rows + -q_rows % 16
    smem = pl.BlockSpec(memory_space=pltpu.SMEM)
    vmem = pl.BlockSpec(memory_space=pltpu.VMEM)
    hbm = pl.BlockSpec(memory_space=pltpu.HBM)
    anywhere = pl.BlockSpec(memory_space=pl.ANY)
    free = pl.BlockSpec()

    own = jnp.concatenate(
        [
            lax.dynamic_slice_in_dim(weight, y * half, half, 0),
            jnp.pad(queries.reshape(q_rows, columns), ((0, q_room - q_rows), (0, 0))),
        ],
        0,
    )
    own, tokens = fence((own, tokens))
    piece = jax.ShapeDtypeStruct((rows, 4 * half), tokens.dtype)
    piece_x, kept, kept_other = pl.pallas_call(
        carve_kernel,
        in_specs=[smem, hbm],
        out_specs=[vmem] * 3,
        out_shape=[piece] * 3,
        scratch_shapes=[pltpu.SemaphoreType.DMA((12,))],
        compiler_params=ALL,
    )(place, tokens)
    middle, outward = [(1, 2), (2, 1)], [(1, 0), (2, 3)]
    near = lax.ppermute(own, "z", [(0, 1), (1, 0), (2, 3), (3, 2)])
    across = lax.ppermute(own, "z", middle)
    tok = lax.ppermute(piece_x, "x", SWAP)

    across_next = lax.ppermute(near, "z", middle)
    out = lax.ppermute(across, "z", outward)
    y_near = lax.ppermute(near, "y", SWAP)

    across_next, out = fence((across_next, out))
    out_next = lax.ppermute(across_next, "z", outward)
    third, y_near = fence((jnp.where(edge, out, across), y_near))
    y_third = lax.ppermute(third, "y", SWAP)

    fourth = jnp.where(edge, out_next, across_next)
    y_fourth = lax.ppermute(fourth, "y", SWAP)
    other = lax.ppermute(tok, "c", SWAP)
    sides = (kept, tok, kept_other, other)

    acc_shape = jax.ShapeDtypeStruct((2, rows, columns), jnp.float32)
    acc = pl.pallas_call(
        functools.partial(early_kernel, half),
        in_specs=[smem] + [free] * 5 + [anywhere] + [free] * 2,
        out_specs=free,
        out_shape=acc_shape,
        scratch_shapes=[pltpu.VMEM((half, columns), weight.dtype), pltpu.SemaphoreType.DMA],
        compiler_params=ROOM,
    )(place, *sides, own, weight, near, y_near)
    acc, line_q, left = pl.pallas_call(
        functools.partial(middle_kernel, half, q_rows),
        in_specs=[smem] + [free] * 10,
        out_specs=[free] * 3,
        out_shape=[
            acc_shape,
            jax.ShapeDtypeStruct((nz, q_rows * columns // HD, HD), queries.dtype),
            jax.ShapeDtypeStruct((2, rows, half), tokens.dtype),
        ],
        compiler_params=ROOM,
    )(place, *sides, acc, own, near, third, fourth, y_third)
    mark = pl.pallas_call(
        mark_kernel,
        in_specs=[anywhere],
        out_specs=vmem,
        out_shape=jax.ShapeDtypeStruct((8, HD), jnp.float32),
        cost_estimate=pl.CostEstimate(flops=8 * 10**9, bytes_accessed=4096, transcendentals=0),
        compiler_params=ROOM,
    )(y_third)
    keep = ((rows, columns), jnp.float32)
    send = ((rows, columns // 2 * 3), jnp.bfloat16)
    send_x = pl.pallas_call(
        functools.partial(send_kernel, half),
        in_specs=[free] * 3 + [anywhere],
        out_specs=free,
        out_shape=jax.ShapeDtypeStruct(*send),
        compiler_params=ROOM,
    )(left, acc, y_fourth, mark)
    keep_here = pl.pallas_call(
        functools.partial(keep_kernel, half),
        in_specs=[free] * 3,
        out_specs=free,
        out_shape=jax.ShapeDtypeStruct(*keep),
        compiler_params=ROOM,
    )(left, acc, y_fourth)
    parts = [keep_here, lax.ppermute(send_x, "x", SWAP)]

    other_q = lax.ppermute(line_q, "x", SWAP)
    asked = jnp.stack([jnp.where(x == 0, line_q, other_q), jnp.where(x == 0, other_q, line_q)], 1)
    heads = columns // (2 * HD)
    asked = asked.reshape(nz, 2, own_q, heads, GROUP, HD).transpose(3, 0, 1, 2, 4, 5)
    asked = asked.reshape(heads, nz * 2 * own_q * GROUP, HD)
    return parts, asked


def attend_kernel(q_ref, bias_ref, pre_ref, *refs):
    keep_ref, *got_refs, new_ref, out_ref = refs
    for g in range(q_ref.shape[0]):
        cut = [slice((2 * g + i) * HD, (2 * g + i + 1) * HD) for i in range(2)]
        sums = [keep_ref[:, at] for at in cut]
        for got in got_refs:
            sums = [s + more for s, more in zip(sums, unpack(got, g))]
        for at, s in zip(cut, sums):
            new_ref[:, at] = s.astype(jnp.bfloat16)
    heads = q_ref.shape[0]
    rows = q_ref.shape[1]
    docs, pref_rows = pre_ref.shape[0], pre_ref.shape[1]
    lane = lax.broadcasted_iota(jnp.int32, (rows, HD), 1)
    contract = (((1,), (1,)), ((), ()))
    stat = jnp.zeros((rows, HD), jnp.float32)
    for g in range(heads):
        key = slice(2 * g * HD, (2 * g + 1) * HD)
        val = slice((2 * g + 1) * HD, (2 * g + 2) * HD)
        q = q_ref[g]
        parts = [(pre_ref[d, :, key], pre_ref[d, :, val]) for d in range(docs)]
        parts.append((new_ref[:, key], new_ref[:, val]))
        scores = []
        at = 0
        for k, _ in parts:
            s = lax.dot_general(q, k, contract, preferred_element_type=jnp.float32)
            s = s * (1.0 / HD**0.5) + bias_ref[:, at : at + k.shape[0]]
            scores.append(s)
            at += k.shape[0]
        peak = functools.reduce(jnp.maximum, [jnp.max(s, axis=1, keepdims=True) for s in scores])
        total = jnp.zeros((rows, 1), jnp.float32)
        mixed = jnp.zeros((rows, HD), jnp.float32)
        for s, (_, v) in zip(scores, parts):
            e = jnp.exp(s - peak)
            total = total + jnp.sum(e, axis=1, keepdims=True)
            mixed = mixed + jnp.dot(e.astype(jnp.bfloat16), v, preferred_element_type=jnp.float32)
        n_quest = rows // GROUP
        out_ref[:, g] = mixed.reshape(n_quest, GROUP, HD)
        stat = jnp.where(lane == 2 * g, peak, jnp.where(lane == 2 * g + 1, total, stat))
    out_ref[:, heads] = stat.reshape(n_quest, GROUP, HD)


def finish_kernel(n_dev, part_ref, out_ref):
    own = part_ref.shape[0] // n_dev
    heads = part_ref.shape[1] - 1
    for r in range(own):
        for g in range(heads):
            peaks = [part_ref[d * own + r, heads, :, 2 * g : 2 * g + 1] for d in range(n_dev)]
            top = functools.reduce(jnp.maximum, peaks)
            total = jnp.zeros((GROUP, 1), jnp.float32)
            mixed = jnp.zeros((GROUP, HD), jnp.float32)
            for d in range(n_dev):
                scale = jnp.exp(peaks[d] - top)
                total = total + scale * part_ref[d * own + r, heads, :, 2 * g + 1 : 2 * g + 2]
                mixed = mixed + scale * part_ref[d * own + r, g]
            done = (mixed / total).astype(jnp.bfloat16)
            for j in range(GROUP):
                at = (g * GROUP + j) * HD
                out_ref[r : r + 1, at : at + HD] = done[j : j + 1]


def shards(tokens, weight, prefix, queries, doc, lists, slots):
    nz = lax.axis_size("z")
    x, z = lax.axis_index("x"), lax.axis_index("z")
    rows = tokens.shape[0]
    heads = weight.shape[1] // (2 * HD)
    own_q = queries.shape[0]

    if nz == 4:
        parts, asked = project(tokens, weight, queries)
    else:
        parts = [dot32(tokens, lax.all_gather(weight, ("z", "x"), axis=0, tiled=True))]
        asked = lax.all_gather(queries, ("z", "x"), axis=0, tiled=True)
        asked = asked.reshape(-1, heads, GROUP, HD).transpose(1, 0, 2, 3).reshape(heads, -1, HD)
    n_quest = asked.shape[1] // GROUP

    pref_rows = prefix.shape[1]
    row_slot = ((z * 2 + x) * rows + jnp.arange(rows, dtype=jnp.int32)) // CLEN
    key_doc = jnp.concatenate(
        [jnp.arange(DOCS * pref_rows, dtype=jnp.int32) // pref_rows, jnp.full((rows,), -1, jnp.int32)]
    )
    key_slot = jnp.concatenate([jnp.full((DOCS * pref_rows,), -1, jnp.int32), row_slot])
    wanted = slots[lists]
    visible = (doc[:, None] == key_doc[None, :]) | jnp.any(
        wanted[:, :, None] == key_slot[None, None, :], axis=1
    )
    bias = jnp.where(visible, 0.0, -jnp.inf).astype(jnp.float32)
    bias = jnp.repeat(bias, GROUP, axis=0)

    new_cache, part = pl.pallas_call(
        attend_kernel,
        out_shape=(
            jax.ShapeDtypeStruct(parts[0].shape, jnp.bfloat16),
            jax.ShapeDtypeStruct((n_quest, heads + 1, GROUP, HD), jnp.float32),
        ),
        compiler_params=ROOM,
    )(asked, bias, prefix, *parts)
    part = lax.all_to_all(part, ("z", "x"), 0, 0, tiled=True)
    attended = pl.pallas_call(
        functools.partial(finish_kernel, 2 * nz),
        out_shape=jax.ShapeDtypeStruct((own_q, heads * GROUP * HD), jnp.bfloat16),
        compiler_params=ROOM,
    )(part)
    return new_cache, attended


def solution(mesh):
    groups, wide, narrow = (mesh.shape[a] for a in ("groups", "wide", "narrow"))
    split = Mesh(mesh.devices.reshape(groups, wide // 2, 2, narrow), ("y", "z", "x", "c"))
    row = ("y", "z", "x")
    placed = (
        P(row, None),
        P(("z", "x"), "c"),
        P(None, row, "c"),
        P(row, "c"),
        P("y"),
        P("y", None),
        P("y"),
    )
    return jax.shard_map(
        shards,
        mesh=split,
        in_specs=placed,
        out_specs=(P(row, "c"), P(row, "c")),
        check_vma=False,
    )
```

```python
import functools

import jax
import jax.numpy as jnp
from jax import lax
from jax.experimental import pallas as pl
from jax.experimental.pallas import tpu as pltpu
from jax.sharding import Mesh
from jax.sharding import PartitionSpec as P

HD = 128
GROUP = 8
CLEN = 512
DOCS = 2
SWAP = [(0, 1), (1, 0)]
ALL = pltpu.CompilerParams(vmem_limit_bytes=60 * 2**20)
ROOM = pltpu.CompilerParams(vmem_limit_bytes=16 * 2**20)


def dot32(a, b):
    return jnp.dot(a, b, preferred_element_type=jnp.float32)


def order_of(z):
    low = z < 2
    return [z, z ^ 1, jnp.where(low, 2, 1), jnp.where(low, 3, 0)]


def carve_kernel(place_ref, tokens, *refs):
    piece_refs, sems = refs[:3], refs[3]
    width = piece_refs[0].shape[1] // 4
    core, x = place_ref[4], place_ref[6]
    copies = []
    for n, (ref, (dx, dc)) in enumerate(zip(piece_refs, ((1, 0), (0, 0), (0, 1)))):
        for i in range(4):
            at = ((place_ref[i] * 2 + (x ^ dx)) * 2 + (core ^ dc)) * width
            copies.append(
                pltpu.make_async_copy(
                    tokens.at[:, pl.ds(pl.multiple_of(at, width), width)],
                    ref.at[:, pl.ds(i * width, width)],
                    sems.at[n * 4 + i],
                )
            )
    for copy in copies:
        copy.start()
    for copy in copies:
        copy.wait()


def half_terms(place_ref, firsts, seconds, index, along_z, along_y):
    width = firsts[0].shape[1] // 4
    cut = slice(index * width, (index + 1) * width)
    same = place_ref[4] == place_ref[7]
    terms = [None] * len(firsts)
    for block, mine in ((along_z, same), (along_y, jnp.logical_not(same))):
        if block is not None:
            for b, (f, s) in enumerate(zip(firsts, seconds)):
                term = dot32(jnp.where(mine, f[:, cut], s[:, cut]), block)
                terms[b] = term if terms[b] is None else terms[b] + term
    return terms


def early_kernel(half, place_ref, *refs):
    firsts, seconds, (own, weight, near, y_near, acc_ref, weight_ref, sem) = refs[:2], refs[2:4], refs[4:]
    load = pltpu.make_async_copy(
        weight.at[pl.ds(pl.multiple_of((1 - place_ref[7]) * half, half), half)], weight_ref, sem
    )
    load.start()
    sums = half_terms(place_ref, firsts, seconds, 1, near[:half], y_near[...])
    load.wait()
    terms = half_terms(place_ref, firsts, seconds, 0, own[:half], weight_ref[...])
    for b in range(2):
        acc_ref[b] = sums[b] + terms[b]


def middle_kernel(half, q_rows, place_ref, *refs):
    firsts, seconds = refs[:2], refs[2:4]
    old_ref, own, near, across, out, across_next, out_next, y_third, acc_ref, line_ref, left_ref = refs[4:]
    third = jnp.where(place_ref[5] == 1, out[...], across[...])
    fourth = jnp.where(place_ref[5] == 1, out_next[...], across_next[...])
    per = own.shape[1] // HD
    for i, block in enumerate((own, near, third, fourth)):
        for r in range(q_rows):
            for h in range(per):
                at = slice(h * HD, (h + 1) * HD)
                line_ref[place_ref[i], r * per + h : r * per + h + 1] = block[half + r : half + r + 1, at]
    sums = half_terms(place_ref, firsts, seconds, 2, third[:half], y_third[...])
    terms = half_terms(place_ref, firsts, seconds, 3, fourth[:half], None)
    width = left_ref.shape[2]
    cut = slice(3 * width, 4 * width)
    other = place_ref[4] != place_ref[7]
    for b in range(2):
        acc_ref[b] = old_ref[b] + sums[b] + terms[b]
        left_ref[b] = jnp.where(other, firsts[b][:, cut], seconds[b][:, cut])


def mark_kernel(given_ref, mark_ref):
    mark_ref[...] = jnp.zeros_like(mark_ref)


def send_kernel(half, left_ref, acc_ref, block_ref, mark_ref, send_ref):
    pack(acc_ref[1] + dot32(left_ref[1], block_ref[...]), send_ref)


def keep_kernel(half, left_ref, acc_ref, block_ref, keep_ref):
    keep_ref[...] = acc_ref[0] + dot32(left_ref[0], block_ref[...])


def pack(part, ref):
    for g in range(part.shape[1] // (2 * HD)):
        key = part[:, 2 * g * HD : (2 * g + 1) * HD]
        high = key.astype(jnp.bfloat16)
        at = 3 * g * HD
        ref[:, at : at + HD] = high
        ref[:, at + HD : at + 2 * HD] = (key - high.astype(jnp.float32)).astype(jnp.bfloat16)
        ref[:, at + 2 * HD : at + 3 * HD] = part[:, (2 * g + 1) * HD : (2 * g + 2) * HD].astype(jnp.bfloat16)


def unpack(ref, g):
    at = 3 * g * HD
    high, low, value = (ref[:, at + i * HD : at + (i + 1) * HD].astype(jnp.float32) for i in range(3))
    return high + low, value


def project(tokens, weight, queries):
    x, y, z, c = (lax.axis_index(a) for a in ("x", "y", "z", "c"))
    rows = tokens.shape[0]
    columns = weight.shape[1]
    half = weight.shape[0] // 2
    nz = 4
    edge = (z == 0) | (z == 3)
    place = jnp.stack([*order_of(z), c, edge, x, y]).astype(jnp.int32)
    fence = lax.optimization_barrier
    own_q, q_width = queries.shape
    q_rows = own_q * q_width // columns
    q_room = q_rows + -q_rows % 16
    smem = pl.BlockSpec(memory_space=pltpu.SMEM)
    vmem = pl.BlockSpec(memory_space=pltpu.VMEM)
    hbm = pl.BlockSpec(memory_space=pltpu.HBM)
    anywhere = pl.BlockSpec(memory_space=pl.ANY)
    free = pl.BlockSpec()

    own = jnp.concatenate(
        [
            lax.dynamic_slice_in_dim(weight, y * half, half, 0),
            jnp.pad(queries.reshape(q_rows, columns), ((0, q_room - q_rows), (0, 0))),
        ],
        0,
    )
    own, tokens = fence((own, tokens))
    piece = jax.ShapeDtypeStruct((rows, 4 * half), tokens.dtype)
    piece_x, kept, kept_other = pl.pallas_call(
        carve_kernel,
        in_specs=[smem, hbm],
        out_specs=[vmem] * 3,
        out_shape=[piece] * 3,
        scratch_shapes=[pltpu.SemaphoreType.DMA((12,))],
        compiler_params=ALL,
    )(place, tokens)
    middle, outward = [(1, 2), (2, 1)], [(1, 0), (2, 3)]
    near = lax.ppermute(own, "z", [(0, 1), (1, 0), (2, 3), (3, 2)])
    across = lax.ppermute(own, "z", middle)
    tok = lax.ppermute(piece_x, "x", SWAP)

    across_next = lax.ppermute(near, "z", middle)
    out = lax.ppermute(across, "z", outward)
    y_near = lax.ppermute(near[:half], "y", SWAP)

    across_next, out = fence((across_next, out))
    out_next = lax.ppermute(across_next, "z", outward)
    third, y_near = fence((jnp.where(edge, out[:half], across[:half]), y_near))
    y_third = lax.ppermute(third, "y", SWAP)

    y_fourth = lax.ppermute(jnp.where(edge, out_next[:half], across_next[:half]), "y", SWAP)
    other = lax.ppermute(tok, "c", SWAP)
    sides = (kept, tok, kept_other, other)

    acc_shape = jax.ShapeDtypeStruct((2, rows, columns), jnp.float32)
    acc = pl.pallas_call(
        functools.partial(early_kernel, half),
        in_specs=[smem] + [free] * 5 + [anywhere] + [free] * 2,
        out_specs=free,
        out_shape=acc_shape,
        scratch_shapes=[pltpu.VMEM((half, columns), weight.dtype), pltpu.SemaphoreType.DMA],
        compiler_params=ROOM,
    )(place, *sides, own, weight, near, y_near)
    acc, line_q, left = pl.pallas_call(
        functools.partial(middle_kernel, half, q_rows),
        in_specs=[smem] + [free] * 12,
        out_specs=[free] * 3,
        out_shape=[
            acc_shape,
            jax.ShapeDtypeStruct((nz, q_rows * columns // HD, HD), queries.dtype),
            jax.ShapeDtypeStruct((2, rows, half), tokens.dtype),
        ],
        compiler_params=ROOM,
    )(place, *sides, acc, own, near, across, out, across_next, out_next, y_third)
    mark = pl.pallas_call(
        mark_kernel,
        in_specs=[anywhere],
        out_specs=vmem,
        out_shape=jax.ShapeDtypeStruct((8, HD), jnp.float32),
        cost_estimate=pl.CostEstimate(flops=8 * 10**9, bytes_accessed=4096, transcendentals=0),
        compiler_params=ROOM,
    )(y_third)
    keep = ((rows, columns), jnp.float32)
    send = ((rows, columns // 2 * 3), jnp.bfloat16)
    send_x = pl.pallas_call(
        functools.partial(send_kernel, half),
        in_specs=[free] * 3 + [anywhere],
        out_specs=free,
        out_shape=jax.ShapeDtypeStruct(*send),
        compiler_params=ROOM,
    )(left, acc, y_fourth, mark)
    keep_here = pl.pallas_call(
        functools.partial(keep_kernel, half),
        in_specs=[free] * 3,
        out_specs=free,
        out_shape=jax.ShapeDtypeStruct(*keep),
        compiler_params=ROOM,
    )(left, acc, y_fourth)
    parts = [keep_here, lax.ppermute(send_x, "x", SWAP)]

    other_q = lax.ppermute(line_q, "x", SWAP)
    asked = jnp.stack([jnp.where(x == 0, line_q, other_q), jnp.where(x == 0, other_q, line_q)], 1)
    heads = columns // (2 * HD)
    asked = asked.reshape(nz, 2, own_q, heads, GROUP, HD).transpose(3, 0, 1, 2, 4, 5)
    asked = asked.reshape(heads, nz * 2 * own_q * GROUP, HD)
    return parts, asked


def attend_kernel(q_ref, bias_ref, pre_ref, *refs):
    keep_ref, *got_refs, new_ref, out_ref = refs
    for g in range(q_ref.shape[0]):
        cut = [slice((2 * g + i) * HD, (2 * g + i + 1) * HD) for i in range(2)]
        sums = [keep_ref[:, at] for at in cut]
        for got in got_refs:
            sums = [s + more for s, more in zip(sums, unpack(got, g))]
        for at, s in zip(cut, sums):
            new_ref[:, at] = s.astype(jnp.bfloat16)
    heads = q_ref.shape[0]
    rows = q_ref.shape[1]
    docs, pref_rows = pre_ref.shape[0], pre_ref.shape[1]
    lane = lax.broadcasted_iota(jnp.int32, (rows, HD), 1)
    contract = (((1,), (1,)), ((), ()))
    stat = jnp.zeros((rows, HD), jnp.float32)
    for g in range(heads):
        key = slice(2 * g * HD, (2 * g + 1) * HD)
        val = slice((2 * g + 1) * HD, (2 * g + 2) * HD)
        q = q_ref[g]
        parts = [(pre_ref[d, :, key], pre_ref[d, :, val]) for d in range(docs)]
        parts.append((new_ref[:, key], new_ref[:, val]))
        scores = []
        at = 0
        for k, _ in parts:
            s = lax.dot_general(q, k, contract, preferred_element_type=jnp.float32)
            s = s * (1.0 / HD**0.5) + bias_ref[:, at : at + k.shape[0]]
            scores.append(s)
            at += k.shape[0]
        peak = functools.reduce(jnp.maximum, [jnp.max(s, axis=1, keepdims=True) for s in scores])
        total = jnp.zeros((rows, 1), jnp.float32)
        mixed = jnp.zeros((rows, HD), jnp.float32)
        for s, (_, v) in zip(scores, parts):
            e = jnp.exp(s - peak)
            total = total + jnp.sum(e, axis=1, keepdims=True)
            mixed = mixed + jnp.dot(e.astype(jnp.bfloat16), v, preferred_element_type=jnp.float32)
        n_quest = rows // GROUP
        out_ref[:, g] = mixed.reshape(n_quest, GROUP, HD)
        stat = jnp.where(lane == 2 * g, peak, jnp.where(lane == 2 * g + 1, total, stat))
    out_ref[:, heads] = stat.reshape(n_quest, GROUP, HD)


def finish_kernel(n_dev, part_ref, out_ref):
    own = part_ref.shape[0] // n_dev
    heads = part_ref.shape[1] - 1
    for r in range(own):
        for g in range(heads):
            peaks = [part_ref[d * own + r, heads, :, 2 * g : 2 * g + 1] for d in range(n_dev)]
            top = functools.reduce(jnp.maximum, peaks)
            total = jnp.zeros((GROUP, 1), jnp.float32)
            mixed = jnp.zeros((GROUP, HD), jnp.float32)
            for d in range(n_dev):
                scale = jnp.exp(peaks[d] - top)
                total = total + scale * part_ref[d * own + r, heads, :, 2 * g + 1 : 2 * g + 2]
                mixed = mixed + scale * part_ref[d * own + r, g]
            done = (mixed / total).astype(jnp.bfloat16)
            for j in range(GROUP):
                at = (g * GROUP + j) * HD
                out_ref[r : r + 1, at : at + HD] = done[j : j + 1]


def shards(tokens, weight, prefix, queries, doc, lists, slots):
    nz = lax.axis_size("z")
    x, z = lax.axis_index("x"), lax.axis_index("z")
    rows = tokens.shape[0]
    heads = weight.shape[1] // (2 * HD)
    own_q = queries.shape[0]

    if nz == 4:
        parts, asked = project(tokens, weight, queries)
    else:
        parts = [dot32(tokens, lax.all_gather(weight, ("z", "x"), axis=0, tiled=True))]
        asked = lax.all_gather(queries, ("z", "x"), axis=0, tiled=True)
        asked = asked.reshape(-1, heads, GROUP, HD).transpose(1, 0, 2, 3).reshape(heads, -1, HD)
    n_quest = asked.shape[1] // GROUP

    pref_rows = prefix.shape[1]
    row_slot = ((z * 2 + x) * rows + jnp.arange(rows, dtype=jnp.int32)) // CLEN
    key_doc = jnp.concatenate(
        [jnp.arange(DOCS * pref_rows, dtype=jnp.int32) // pref_rows, jnp.full((rows,), -1, jnp.int32)]
    )
    key_slot = jnp.concatenate([jnp.full((DOCS * pref_rows,), -1, jnp.int32), row_slot])
    wanted = slots[lists]
    visible = (doc[:, None] == key_doc[None, :]) | jnp.any(
        wanted[:, :, None] == key_slot[None, None, :], axis=1
    )
    bias = jnp.where(visible, 0.0, -jnp.inf).astype(jnp.float32)
    bias = jnp.repeat(bias, GROUP, axis=0)

    new_cache, part = pl.pallas_call(
        attend_kernel,
        out_shape=(
            jax.ShapeDtypeStruct(parts[0].shape, jnp.bfloat16),
            jax.ShapeDtypeStruct((n_quest, heads + 1, GROUP, HD), jnp.float32),
        ),
        compiler_params=ROOM,
    )(asked, bias, prefix, *parts)
    part = lax.all_to_all(part, ("z", "x"), 0, 0, tiled=True)
    attended = pl.pallas_call(
        functools.partial(finish_kernel, 2 * nz),
        out_shape=jax.ShapeDtypeStruct((own_q, heads * GROUP * HD), jnp.bfloat16),
        compiler_params=ROOM,
    )(part)
    return new_cache, attended


def solution(mesh):
    groups, wide, narrow = (mesh.shape[a] for a in ("groups", "wide", "narrow"))
    split = Mesh(mesh.devices.reshape(groups, wide // 2, 2, narrow), ("y", "z", "x", "c"))
    row = ("y", "z", "x")
    placed = (
        P(row, None),
        P(("z", "x"), "c"),
        P(None, row, "c"),
        P(row, "c"),
        P("y"),
        P("y", None),
        P("y"),
    )
    return jax.shard_map(
        shards,
        mesh=split,
        in_specs=placed,
        out_specs=(P(row, "c"), P(row, "c")),
        check_vma=False,
    )
```

```python
import functools

import jax
import jax.numpy as jnp
from jax import lax
from jax.experimental import pallas as pl
from jax.experimental.pallas import tpu as pltpu
from jax.sharding import Mesh
from jax.sharding import PartitionSpec as P

HD = 128
GROUP = 8
CLEN = 512
DOCS = 2
SWAP = [(0, 1), (1, 0)]
ALL = pltpu.CompilerParams(vmem_limit_bytes=60 * 2**20)
ROOM = pltpu.CompilerParams(vmem_limit_bytes=16 * 2**20)


def dot32(a, b):
    return jnp.dot(a, b, preferred_element_type=jnp.float32)


def order_of(z):
    low = z < 2
    return [z, z ^ 1, jnp.where(low, 2, 1), jnp.where(low, 3, 0)]


def carve_kernel(place_ref, tokens, *refs):
    piece_refs, sems = refs[:3], refs[3]
    width = piece_refs[0].shape[1] // 4
    core, x = place_ref[4], place_ref[6]
    copies = []
    for n, (ref, (dx, dc)) in enumerate(zip(piece_refs, ((1, 0), (0, 0), (0, 1)))):
        for i in range(4):
            at = ((place_ref[i] * 2 + (x ^ dx)) * 2 + (core ^ dc)) * width
            copies.append(
                pltpu.make_async_copy(
                    tokens.at[:, pl.ds(pl.multiple_of(at, width), width)],
                    ref.at[:, pl.ds(i * width, width)],
                    sems.at[n * 4 + i],
                )
            )
    for copy in copies:
        copy.start()
    for copy in copies:
        copy.wait()


def half_terms(place_ref, firsts, seconds, index, along_z, along_y):
    width = firsts[0].shape[1] // 4
    cut = slice(index * width, (index + 1) * width)
    same = place_ref[4] == place_ref[7]
    terms = [None] * len(firsts)
    for block, mine in ((along_z, same), (along_y, jnp.logical_not(same))):
        if block is not None:
            for b, (f, s) in enumerate(zip(firsts, seconds)):
                term = dot32(jnp.where(mine, f[:, cut], s[:, cut]), block)
                terms[b] = term if terms[b] is None else terms[b] + term
    return terms


def early_kernel(half, place_ref, *refs):
    firsts, seconds, (own, weight, near, y_near, acc_ref, weight_ref, sem) = refs[:2], refs[2:4], refs[4:]
    load = pltpu.make_async_copy(
        weight.at[pl.ds(pl.multiple_of((1 - place_ref[7]) * half, half), half)], weight_ref, sem
    )
    load.start()
    sums = half_terms(place_ref, firsts, seconds, 1, near[:half], y_near[...])
    load.wait()
    terms = half_terms(place_ref, firsts, seconds, 0, own[:half], weight_ref[...])
    for b in range(2):
        acc_ref[b] = sums[b] + terms[b]


def middle_kernel(half, q_rows, place_ref, *refs):
    firsts, seconds = refs[:2], refs[2:4]
    old_ref, own, near, across, out, across_next, out_next, y_third, acc_ref, line_ref, left_ref = refs[4:]
    third = jnp.where(place_ref[5] == 1, out[...], across[...])
    fourth = jnp.where(place_ref[5] == 1, out_next[...], across_next[...])
    per = own.shape[1] // HD
    for i, block in enumerate((own, near, third, fourth)):
        for r in range(q_rows):
            for h in range(per):
                at = slice(h * HD, (h + 1) * HD)
                line_ref[place_ref[i], r * per + h : r * per + h + 1] = block[half + r : half + r + 1, at]
    sums = half_terms(place_ref, firsts, seconds, 2, third[:half], y_third[...])
    terms = half_terms(place_ref, firsts, seconds, 3, fourth[:half], None)
    width = left_ref.shape[2]
    cut = slice(3 * width, 4 * width)
    other = place_ref[4] != place_ref[7]
    for b in range(2):
        acc_ref[b] = old_ref[b] + sums[b] + terms[b]
        left_ref[b] = jnp.where(other, firsts[b][:, cut], seconds[b][:, cut])


def mark_kernel(given_ref, mark_ref):
    mark_ref[...] = jnp.zeros_like(mark_ref)


def send_kernel(half, left_ref, acc_ref, block_ref, mark_ref, send_ref):
    pack(acc_ref[1] + dot32(left_ref[1], block_ref[...]), send_ref)


def keep_kernel(half, left_ref, acc_ref, block_ref, keep_ref):
    keep_ref[...] = acc_ref[0] + dot32(left_ref[0], block_ref[...])


def pack(part, ref):
    for g in range(part.shape[1] // (2 * HD)):
        key = part[:, 2 * g * HD : (2 * g + 1) * HD]
        high = key.astype(jnp.bfloat16)
        at = 3 * g * HD
        ref[:, at : at + HD] = high
        ref[:, at + HD : at + 2 * HD] = (key - high.astype(jnp.float32)).astype(jnp.bfloat16)
        ref[:, at + 2 * HD : at + 3 * HD] = part[:, (2 * g + 1) * HD : (2 * g + 2) * HD].astype(jnp.bfloat16)


def unpack(ref, g):
    at = 3 * g * HD
    high, low, value = (ref[:, at + i * HD : at + (i + 1) * HD].astype(jnp.float32) for i in range(3))
    return high + low, value


def project(tokens, weight, queries):
    x, y, z, c = (lax.axis_index(a) for a in ("x", "y", "z", "c"))
    rows = tokens.shape[0]
    columns = weight.shape[1]
    half = weight.shape[0] // 2
    nz = 4
    edge = (z == 0) | (z == 3)
    place = jnp.stack([*order_of(z), c, edge, x, y]).astype(jnp.int32)
    fence = lax.optimization_barrier
    own_q, q_width = queries.shape
    q_rows = own_q * q_width // columns
    q_room = q_rows + -q_rows % 16
    smem = pl.BlockSpec(memory_space=pltpu.SMEM)
    vmem = pl.BlockSpec(memory_space=pltpu.VMEM)
    hbm = pl.BlockSpec(memory_space=pltpu.HBM)
    anywhere = pl.BlockSpec(memory_space=pl.ANY)
    free = pl.BlockSpec()

    own = jnp.concatenate(
        [
            lax.dynamic_slice_in_dim(weight, y * half, half, 0),
            jnp.pad(queries.reshape(q_rows, columns), ((0, q_room - q_rows), (0, 0))),
        ],
        0,
    )
    own, tokens = fence((own, tokens))
    piece = jax.ShapeDtypeStruct((rows, 4 * half), tokens.dtype)
    piece_x, kept, kept_other = pl.pallas_call(
        carve_kernel,
        in_specs=[smem, hbm],
        out_specs=[vmem] * 3,
        out_shape=[piece] * 3,
        scratch_shapes=[pltpu.SemaphoreType.DMA((12,))],
        compiler_params=ALL,
    )(place, tokens)
    middle, outward = [(1, 2), (2, 1)], [(1, 0), (2, 3)]
    near = lax.ppermute(own, "z", [(0, 1), (1, 0), (2, 3), (3, 2)])
    across = lax.ppermute(own, "z", middle)
    tok = lax.ppermute(piece_x, "x", SWAP)

    across_next = lax.ppermute(near, "z", middle)
    out = lax.ppermute(across, "z", outward)
    y_near = lax.ppermute(near[:half], "y", SWAP)

    across_next, out = fence((across_next, out))
    out_next = lax.ppermute(across_next, "z", outward)
    third, y_near = fence((jnp.where(edge, out[:half], across[:half]), y_near))
    y_third = lax.ppermute(third, "y", SWAP)

    y_fourth = lax.ppermute(jnp.where(edge, out_next[:half], across_next[:half]), "y", SWAP)
    other = lax.ppermute(tok, "c", SWAP)
    sides = (kept, tok, kept_other, other)

    acc_shape = jax.ShapeDtypeStruct((2, rows, columns), jnp.float32)
    acc = pl.pallas_call(
        functools.partial(early_kernel, half),
        in_specs=[smem] + [free] * 5 + [anywhere] + [free] * 2,
        out_specs=free,
        out_shape=acc_shape,
        scratch_shapes=[pltpu.VMEM((half, columns), weight.dtype), pltpu.SemaphoreType.DMA],
        compiler_params=ROOM,
    )(place, *sides, own, weight, near, y_near)
    acc, line_q, left = pl.pallas_call(
        functools.partial(middle_kernel, half, q_rows),
        in_specs=[smem] + [free] * 12,
        out_specs=[free] * 3,
        out_shape=[
            acc_shape,
            jax.ShapeDtypeStruct((nz, q_rows * columns // HD, HD), queries.dtype),
            jax.ShapeDtypeStruct((2, rows, half), tokens.dtype),
        ],
        compiler_params=ROOM,
    )(place, *sides, acc, own, near, across, out, across_next, out_next, y_third)
    mark = pl.pallas_call(
        mark_kernel,
        in_specs=[anywhere],
        out_specs=vmem,
        out_shape=jax.ShapeDtypeStruct((8, HD), jnp.float32),
        cost_estimate=pl.CostEstimate(flops=11 * 10**9, bytes_accessed=4096, transcendentals=0),
        compiler_params=ROOM,
    )(y_third)
    keep = ((rows, columns), jnp.float32)
    send = ((rows, columns // 2 * 3), jnp.bfloat16)
    send_x = pl.pallas_call(
        functools.partial(send_kernel, half),
        in_specs=[free] * 3 + [anywhere],
        out_specs=free,
        out_shape=jax.ShapeDtypeStruct(*send),
        compiler_params=ROOM,
    )(left, acc, y_fourth, mark)
    keep_here = pl.pallas_call(
        functools.partial(keep_kernel, half),
        in_specs=[free] * 3,
        out_specs=free,
        out_shape=jax.ShapeDtypeStruct(*keep),
        compiler_params=ROOM,
    )(left, acc, y_fourth)
    parts = [keep_here, lax.ppermute(send_x, "x", SWAP)]

    other_q = lax.ppermute(line_q, "x", SWAP)
    asked = jnp.stack([jnp.where(x == 0, line_q, other_q), jnp.where(x == 0, other_q, line_q)], 1)
    heads = columns // (2 * HD)
    asked = asked.reshape(nz, 2, own_q, heads, GROUP, HD).transpose(3, 0, 1, 2, 4, 5)
    asked = asked.reshape(heads, nz * 2 * own_q * GROUP, HD)
    return parts, asked


CONTRACT = (((1,), (1,)), ((), ()))


def scored(q, key, bias):
    return lax.dot_general(q, key, CONTRACT, preferred_element_type=jnp.float32) * (1.0 / HD**0.5) + bias


def row_sum(e):
    return jnp.sum(e, axis=1, keepdims=True)


def prefix_kernel(q_ref, bias_ref, pre_ref, mixed_ref, stat_ref):
    heads, rows = q_ref.shape[0], q_ref.shape[1]
    docs, pref_rows = pre_ref.shape[0], pre_ref.shape[1]
    lane = lax.broadcasted_iota(jnp.int32, (rows, HD), 1)
    stat = jnp.zeros((rows, HD), jnp.float32)
    for g in range(heads):
        key = slice(2 * g * HD, (2 * g + 1) * HD)
        val = slice((2 * g + 1) * HD, (2 * g + 2) * HD)
        scores = [
            scored(q_ref[g], pre_ref[d, :, key], bias_ref[:, d * pref_rows : (d + 1) * pref_rows])
            for d in range(docs)
        ]
        peak = functools.reduce(jnp.maximum, [jnp.max(s, axis=1, keepdims=True) for s in scores])
        terms = [jnp.exp(s - peak) for s in scores]
        total = functools.reduce(jnp.add, [row_sum(e) for e in terms])
        mixed_ref[g] = functools.reduce(
            jnp.add, [dot32(e.astype(jnp.bfloat16), pre_ref[d, :, val]) for d, e in enumerate(terms)]
        )
        stat = jnp.where(lane == 2 * g, peak, jnp.where(lane == 2 * g + 1, total, stat))
    stat_ref[...] = stat


def attend_kernel(q_ref, bias_ref, mixed_ref, stat_ref, *refs):
    keep_ref, *got_refs, new_ref, out_ref = refs
    heads, rows = q_ref.shape[0], q_ref.shape[1]
    n_quest = rows // GROUP
    start = bias_ref.shape[1] - new_ref.shape[0]
    lane = lax.broadcasted_iota(jnp.int32, (rows, HD), 1)
    stat = jnp.zeros((rows, HD), jnp.float32)
    for g in range(heads):
        cut = [slice((2 * g + i) * HD, (2 * g + i + 1) * HD) for i in range(2)]
        sums = [keep_ref[:, at] for at in cut]
        for got in got_refs:
            sums = [s + more for s, more in zip(sums, unpack(got, g))]
        key, value = (s.astype(jnp.bfloat16) for s in sums)
        new_ref[:, cut[0]] = key
        new_ref[:, cut[1]] = value
        score = scored(q_ref[g], key, bias_ref[:, start:])
        before = stat_ref[:, 2 * g : 2 * g + 1]
        peak = jnp.maximum(before, jnp.max(score, axis=1, keepdims=True))
        scale = jnp.exp(before - peak)
        e = jnp.exp(score - peak)
        total = scale * stat_ref[:, 2 * g + 1 : 2 * g + 2] + row_sum(e)
        mixed = scale * mixed_ref[g] + dot32(e.astype(jnp.bfloat16), value)
        out_ref[:, g] = mixed.reshape(n_quest, GROUP, HD)
        stat = jnp.where(lane == 2 * g, peak, jnp.where(lane == 2 * g + 1, total, stat))
    out_ref[:, heads] = stat.reshape(n_quest, GROUP, HD)


def finish_kernel(n_dev, part_ref, out_ref):
    own = part_ref.shape[0] // n_dev
    heads = part_ref.shape[1] - 1
    for r in range(own):
        for g in range(heads):
            peaks = [part_ref[d * own + r, heads, :, 2 * g : 2 * g + 1] for d in range(n_dev)]
            top = functools.reduce(jnp.maximum, peaks)
            total = jnp.zeros((GROUP, 1), jnp.float32)
            mixed = jnp.zeros((GROUP, HD), jnp.float32)
            for d in range(n_dev):
                scale = jnp.exp(peaks[d] - top)
                total = total + scale * part_ref[d * own + r, heads, :, 2 * g + 1 : 2 * g + 2]
                mixed = mixed + scale * part_ref[d * own + r, g]
            done = (mixed / total).astype(jnp.bfloat16)
            for j in range(GROUP):
                at = (g * GROUP + j) * HD
                out_ref[r : r + 1, at : at + HD] = done[j : j + 1]


def shards(tokens, weight, prefix, queries, doc, lists, slots):
    nz = lax.axis_size("z")
    x, z = lax.axis_index("x"), lax.axis_index("z")
    rows = tokens.shape[0]
    heads = weight.shape[1] // (2 * HD)
    own_q = queries.shape[0]

    if nz == 4:
        parts, asked = project(tokens, weight, queries)
    else:
        parts = [dot32(tokens, lax.all_gather(weight, ("z", "x"), axis=0, tiled=True))]
        asked = lax.all_gather(queries, ("z", "x"), axis=0, tiled=True)
        asked = asked.reshape(-1, heads, GROUP, HD).transpose(1, 0, 2, 3).reshape(heads, -1, HD)
    n_quest = asked.shape[1] // GROUP

    pref_rows = prefix.shape[1]
    row_slot = ((z * 2 + x) * rows + jnp.arange(rows, dtype=jnp.int32)) // CLEN
    key_doc = jnp.concatenate(
        [jnp.arange(DOCS * pref_rows, dtype=jnp.int32) // pref_rows, jnp.full((rows,), -1, jnp.int32)]
    )
    key_slot = jnp.concatenate([jnp.full((DOCS * pref_rows,), -1, jnp.int32), row_slot])
    wanted = slots[lists]
    visible = (doc[:, None] == key_doc[None, :]) | jnp.any(
        wanted[:, :, None] == key_slot[None, None, :], axis=1
    )
    bias = jnp.where(visible, 0.0, -jnp.inf).astype(jnp.float32)
    bias = jnp.repeat(bias, GROUP, axis=0)

    prefix_part = pl.pallas_call(
        prefix_kernel,
        out_shape=(
            jax.ShapeDtypeStruct((heads, n_quest * GROUP, HD), jnp.float32),
            jax.ShapeDtypeStruct((n_quest * GROUP, HD), jnp.float32),
        ),
        compiler_params=ROOM,
    )(asked, bias, prefix)
    new_cache, part = pl.pallas_call(
        attend_kernel,
        out_shape=(
            jax.ShapeDtypeStruct(parts[0].shape, jnp.bfloat16),
            jax.ShapeDtypeStruct((n_quest, heads + 1, GROUP, HD), jnp.float32),
        ),
        compiler_params=ROOM,
    )(asked, bias, *prefix_part, *parts)
    part = lax.all_to_all(part, ("z", "x"), 0, 0, tiled=True)
    attended = pl.pallas_call(
        functools.partial(finish_kernel, 2 * nz),
        out_shape=jax.ShapeDtypeStruct((own_q, heads * GROUP * HD), jnp.bfloat16),
        compiler_params=ROOM,
    )(part)
    return new_cache, attended


def solution(mesh):
    groups, wide, narrow = (mesh.shape[a] for a in ("groups", "wide", "narrow"))
    split = Mesh(mesh.devices.reshape(groups, wide // 2, 2, narrow), ("y", "z", "x", "c"))
    row = ("y", "z", "x")
    placed = (
        P(row, None),
        P(("z", "x"), "c"),
        P(None, row, "c"),
        P(row, "c"),
        P("y"),
        P("y", None),
        P("y"),
    )
    return jax.shard_map(
        shards,
        mesh=split,
        in_specs=placed,
        out_specs=(P(row, "c"), P(row, "c")),
        check_vma=False,
    )
```
